256 devices in a mesh: dp: 32 (over x, z), tensor: 8 (over y, core).
Axes of the slice: x: 4, y: 4, z: 8, core: 2. Of those that a mesh axis runs over, the one named last changes fastest.
Arguments:
- tokens: bfloat16 [8192, 4096], P('dp', 'tensor'), may hold values from -17 to 17
- cotangent: bfloat16 [8192, 17408], P('dp', 'tensor'), may hold values from -6 to 6
- weight_blocks: bfloat16 [7168, 4096], P('tensor'), may hold values from -0.09375 to 0.09375
- block_rows: int32 [7168], P('tensor'), may hold values from 0 to 63, as said below
- block_slots: int32 [7168], P('tensor'), may hold values from 0 to 33, as said below
Outputs:
- hidden: bfloat16 [8192, 17408], P('dp', 'tensor')
- input_grads: bfloat16 [8192, 4096], P('dp', 'tensor')
- curvature: float32 [7168, 4096], P('tensor', 'dp')
The draws below stay inside these ranges and needn't reach their ends.
Inputs may be any that keep to these rules, and one draw needn't show every extreme that they name: On each tensor device the pairs (block_slots, block_rows) of its 896 blocks are distinct and listed by slot, then by row. `block_slots`: A slot holds 0, 16 or 48 of its device's blocks; on half of the tensor devices every slot holds some.
All inputs are finite; a program needn't handle non-finite values.
Results may differ from the reference program's by a relative error of at most 0.013.
Values may be sent and summed in bfloat16 or wider, within the bound.
A program may use at most 320 MiB of HBM per device.

```python
import jax
import jax.numpy as jnp
from jax import lax

D = 4096
BLK = 64
TOKENS = 8192
RB = 64
CPD = 28
SPREAD = 3
SLOTS = 34
KEPT_DEV = 896
KEPT = 7168
COLS = 17408
ENTRIES = 4096
N_TENSOR = 8


def block_layout(key):
    kinds_key, rows_key, type_key = jax.random.split(key, 3)
    sparse_rows = RB // 4
    dense_rows = 3 * RB // 4
    dense_narrow = CPD // 2 + SPREAD
    sparse_narrow = CPD // 2 - 3 * SPREAD
    dense_full = CPD // 2 - SPREAD
    slot_range = jnp.arange(SLOTS, dtype=jnp.int32)
    narrow_counts = jnp.where(slot_range < dense_narrow, dense_rows, jnp.where(slot_range < dense_narrow + sparse_narrow, sparse_rows, 0))
    full_counts = jnp.where(slot_range < dense_full, dense_rows, sparse_rows)
    type_order = jax.random.permutation(type_key, N_TENSOR)
    is_narrow = (type_order % 2 == 0)[:, None]
    counts = jnp.where(is_narrow, narrow_counts[None, :], full_counts[None, :]).astype(jnp.int32)

    def shuffle_slots(slot_key, slot_counts):
        return jax.random.permutation(slot_key, slot_counts)
    counts = jax.vmap(shuffle_slots)(jax.random.split(kinds_key, N_TENSOR), counts)

    def order_rows(row_key):
        return jax.random.permutation(row_key, RB)
    row_orders = jax.vmap(order_rows)(jax.random.split(rows_key, N_TENSOR * SLOTS))
    row_ranks = jnp.argsort(row_orders, axis=1).reshape(N_TENSOR, SLOTS, RB)
    keep_mask = row_ranks < counts[:, :, None]

    def listing(device_mask):
        flat_mask = device_mask.reshape(SLOTS * RB)
        positions = jnp.argsort(jnp.where(flat_mask, 0, 1).astype(jnp.int32), stable=True)[:KEPT_DEV]
        return ((positions % RB).astype(jnp.int32), (positions // RB).astype(jnp.int32))
    rows_out, slots_out = jax.vmap(listing)(keep_mask)
    return (rows_out.reshape(KEPT), slots_out.reshape(KEPT))


def draw_block_rows(key, part):
    rows_out, slots_out = block_layout(key)
    return rows_out


def draw_block_slots(key, part):
    rows_out, slots_out = block_layout(key)
    return slots_out


def draw_tokens(key, part):
    key = jax.random.fold_in(key, 11)
    base_key, row_key, column_key = jax.random.split(key, 3)
    column_scale = jnp.exp(jax.random.uniform(column_key, (1, D), jnp.float32, -0.5, 0.5))
    base_values = jnp.clip(jax.random.normal(base_key, (TOKENS, D), jnp.float32), -5.0, 5.0)
    row_scale = jnp.exp(jax.random.uniform(row_key, (TOKENS, 1), jnp.float32, -1.15, 1.15))
    return (base_values * row_scale * column_scale / 1.6).astype(jnp.bfloat16)


def steps_of(rng, dims, shards, smallest, high):
    factor_of = 1.0
    for axis_at, parts in shards:
        heights = jax.random.uniform(jax.random.fold_in(jax.random.fold_in(rng, 6), axis_at), (parts,), jnp.float32, smallest / len(shards), high / len(shards))
        factor_of = factor_of * jnp.repeat(jnp.exp(heights), dims[axis_at] // parts).reshape((-1,) + (1,) * (len(dims) - 1 - axis_at))
    return factor_of


def noise(key, shape, width, limit, cuts=(), kind=jnp.bfloat16):
    result = width * jax.random.normal(key, shape, jnp.float32)
    if cuts:
        result = result * steps_of(key, shape, cuts, -0.22, 0.18)
    return jnp.clip(result, -limit, limit).astype(kind)


def setup_inputs(seed: int = 0) -> dict:
    key_of = jax.random.split(jax.random.key(seed), 6)
    tokens = draw_tokens(jax.random.fold_in(key_of[5], 71), 0)
    cotangent = noise(key_of[1], (TOKENS, COLS), 1.0, 6.0, ((0, 32), (1, 8)))
    weight_blocks = noise(key_of[2], (KEPT, ENTRIES), D ** -0.5, 0.09375, ((0, 8),))
    block_rows = draw_block_rows(jax.random.fold_in(key_of[5], 71), 0)
    block_slots = draw_block_slots(jax.random.fold_in(key_of[5], 71), 0)
    return {"tokens": tokens, "cotangent": cotangent, "weight_blocks": weight_blocks, "block_rows": block_rows, "block_slots": block_slots}


def reference(tokens, cotangent, weight_blocks, block_rows, block_slots):
    count_tokens = tokens.shape[0]
    squared_in = (tokens.astype(jnp.float32) * tokens.astype(jnp.float32)).astype(jnp.bfloat16)
    squared_back = (cotangent.astype(jnp.float32) * cotangent.astype(jnp.float32)).astype(jnp.bfloat16)
    owner_device = jnp.arange(KEPT, dtype=jnp.int32) // KEPT_DEV
    columns = (owner_device * SLOTS + block_slots.astype(jnp.int32)).astype(jnp.int32)

    def visit_block(carry, pieces):
        hidden_sum, input_sum = carry
        flat_weight, row_index, column = pieces
        weight = flat_weight.reshape(BLK, BLK)
        row_start = (row_index * BLK).astype(jnp.int32)
        col_start = (column * BLK).astype(jnp.int32)
        row_slice = lax.dynamic_slice_in_dim(tokens, row_start, BLK, 1)
        back_slice = lax.dynamic_slice_in_dim(cotangent, col_start, BLK, 1)
        old_hidden = lax.dynamic_slice_in_dim(hidden_sum, col_start, BLK, 1)
        new_hidden = old_hidden + jnp.dot(row_slice, weight, preferred_element_type=jnp.float32)
        hidden_sum = lax.dynamic_update_slice_in_dim(hidden_sum, new_hidden, col_start, 1)
        old_input = lax.dynamic_slice_in_dim(input_sum, row_start, BLK, 1)
        new_input = old_input + jnp.dot(back_slice, weight.T, preferred_element_type=jnp.float32)
        input_sum = lax.dynamic_update_slice_in_dim(input_sum, new_input, row_start, 1)
        square_rows = lax.dynamic_slice_in_dim(squared_in, row_start, BLK, 1)
        square_cols = lax.dynamic_slice_in_dim(squared_back, col_start, BLK, 1)
        local_sum = jnp.dot(square_rows.T, square_cols, preferred_element_type=jnp.float32)
        return (hidden_sum, input_sum), local_sum.reshape(BLK * BLK) / TOKENS

    initial = (jnp.zeros((count_tokens, COLS), jnp.float32), jnp.zeros((count_tokens, D), jnp.float32))
    (hidden_sum, input_sum), curvature = lax.scan(visit_block, initial, (weight_blocks, block_rows.astype(jnp.int32), columns))
    return hidden_sum.astype(jnp.bfloat16), input_sum.astype(jnp.bfloat16), curvature
```

```python
import functools

import jax
import jax.numpy as jnp
from jax import lax
from jax.experimental import pallas as pl
from jax.experimental.pallas import tpu as pltpu
from jax.sharding import PartitionSpec as P

MESH = pl.DeviceIdType.MESH
BF = jnp.bfloat16
F32 = jnp.float32

NX, NZ, NY = 4, 8, 4
T = 256
F = 512
SLOTS = 34
PAIRS = 17
COLS = 2176
KEPT = 896
GROUPS = 56
HALF = KEPT // 2
REL_ORDER = (0, 1, 3, 2)


def dot(a, b):
    return jnp.dot(a, b, preferred_element_type=F32)


def dot_nt(a, b):
    return lax.dot_general(a, b, (((1,), (1,)), ((), ())), preferred_element_type=F32)


def square(v):
    w = v.astype(F32)
    return (w * w).astype(BF)


def kernel(
    tok, cot_hbm, wb_hbm, onehot, pick, slot_group, group_slot,
    hid, grads, curv,
    wb0, wb1, w, cotv, xf, xq, x2t, acc, gbuf, y, rp, rm, bp, bcore, by,
    loc_sem, xs, xr, a_s, ar, ts, tr, tcs, tcr, qs, qr, qcs, qcr, bcs, bcr, bys, byr, zps, zpr, zms, zmr,
):
    dp = lax.axis_index("dp")
    te = lax.axis_index("tensor")
    px = dp // NZ
    pz = lax.rem(dp, NZ)
    py = te // 2
    pc = lax.rem(te, 2)

    def at_x(d):
        return (lax.rem(px + d, NX) * NZ + pz, te)

    def at_z(d):
        return (px * NZ + lax.rem(pz + d, NZ), te)

    def at_y(d):
        return (dp, lax.rem(py + d, NY) * 2 + pc)

    other = (dp, py * 2 + (1 - pc))

    def send(src, dst, ssem, rsem, where):
        return pltpu.make_async_remote_copy(
            src_ref=src, dst_ref=dst, send_sem=ssem, recv_sem=rsem,
            device_id=where, device_id_type=MESH,
        )

    load_cot = pltpu.make_async_copy(cot_hbm, cotv.at[0], loc_sem.at[0])
    load_cot.start()

    def load_wb(kk, slot):
        return pltpu.make_async_copy(
            wb_hbm.at[:, :, pl.ds(pl.multiple_of(kk * 512, 512), 512)],
            (wb0, wb1)[slot].at[pl.ds(0, GROUPS)],
            loc_sem.at[1 + slot],
        )

    load_wb(0, 0).start()
    load_wb(1, 1).start()

    barrier = pltpu.get_barrier_semaphore()
    peers = [at_x(1), at_x(2), at_x(3), at_y(1), at_y(2), at_y(3), other, at_z(1), at_z(7)]
    for who in peers:
        pl.semaphore_signal(barrier, inc=1, device_id=who, device_id_type=MESH)

    fi = lax.broadcasted_iota(jnp.int32, (F, F), 0)
    ci = lax.broadcasted_iota(jnp.int32, (F, F), 1)
    perm = ((fi // 64 == ci % 8) & (fi % 64 == ci // 8)).astype(F32).astype(BF)
    xp = dot(tok[...], perm).astype(BF)
    for q in range(4):
        xf[te, q] = xp[:, q * 128 : (q + 1) * 128]
    wb0[GROUPS:, :, :] = jnp.zeros((4, 16, 512), BF)
    wb1[GROUPS:, :, :] = jnp.zeros((4, 16, 512), BF)

    pl.semaphore_wait(barrier, len(peers))

    a2a = []
    for d in (1, 2, 3):
        a2a.append(send(xf.at[te, lax.rem(px + d, NX)], xq.at[te, 3 - d], a_s.at[3 - d], ar.at[3 - d], at_x(d)))
    for c in a2a:
        c.start()
    tok_y = [send(xf.at[te], xf.at[te], ts.at[d - 1], tr.at[d - 1], at_y(d)) for d in (1, 2, 3)]
    for c in tok_y:
        c.start()
    tok_core = [send(xf.at[te], xf.at[te], tcs.at[0], tcr.at[0], other)]
    tok_core[0].start()

    load_cot.wait()
    top, bot = pl.ds(0, 128), pl.ds(128, 128)
    cx = [
        send(cotv.at[0, top], cotv.at[3, top], xs.at[0], xr.at[0], at_x(1)),
        send(cotv.at[0, bot], cotv.at[1, bot], xs.at[1], xr.at[1], at_x(3)),
        send(cotv.at[0, bot], cotv.at[3, bot], xs.at[2], xr.at[2], at_x(1)),
        send(cotv.at[0, top], cotv.at[1, top], xs.at[3], xr.at[3], at_x(3)),
    ]
    for c in cx:
        c.start()

    low = lax.broadcasted_iota(jnp.int32, (64, 128), 1) < 64

    def expand_group(q, ns, kk, slot):
        lhs = onehot[pl.ds(pl.multiple_of(q * 256, 128), ns * 64), pl.ds(0, ns * 64)]
        rhs = jnp.concatenate(
            [(wb0, wb1)[slot][pl.ds(slot_group[q * 4 + i], 4)].reshape(64, 512) for i in range(ns)], axis=0
        )
        out = dot(lhs, rhs)
        for k4 in range(4):
            for pair in range(ns // 2):
                a = out[pair * 128 : pair * 128 + 64, k4 * 128 : k4 * 128 + 128]
                b = out[pair * 128 + 64 : pair * 128 + 128, k4 * 128 : k4 * 128 + 128]
                p0 = jnp.where(low, a, pltpu.roll(b, 64, 1)).reshape(8, 1, 8, 128)
                p1 = jnp.where(low, pltpu.roll(a, 64, 1), b).reshape(8, 1, 8, 128)
                tile = jnp.concatenate([p0, p1], axis=1).reshape(8, 16, 128).astype(BF)
                w[:, kk * 4 + k4, :, pl.ds(pl.multiple_of(q * 256 + pair * 128, 128), 128)] = tile

    def expand_step(kk, slot):
        load_wb(kk, slot).wait()

        def group(q, carry):
            expand_group(q, 4, kk, slot)
            return carry

        lax.fori_loop(0, 8, group, 0)
        expand_group(8, 2, kk, slot)

    def expand_two(i, carry):
        for slot in range(2):
            expand_step(i * 2 + slot, slot)
            load_wb(i * 2 + 2 + slot, slot).start()
        return carry

    lax.fori_loop(0, 2, expand_two, 0)

    for c in a2a:
        c.wait_recv()
    xq_y = [send(xq.at[te], xq.at[te], qs.at[d - 1], qr.at[d - 1], at_y(d)) for d in (1, 2, 3)]
    for c in xq_y:
        c.start()
    xq_core = [send(xq.at[te], xq.at[te], qcs.at[0], qcr.at[0], other)]
    xq_core[0].start()

    lax.fori_loop(2, 3, expand_two, 0)
    for slot in range(2):
        expand_step(6 + slot, slot)

    def relay(buf, copies, core, ssem, rsem):
        for d in (1, 2, 3):
            copies[d - 1].wait_recv()
            src = lax.rem(py + NY - d, NY) * 2 + pc
            c = send(buf.at[src], buf.at[src], ssem.at[d], rsem.at[d], other)
            c.start()
            core.append(c)

    relay(xf, tok_y, tok_core, tcs, tcr)

    def back(j, carry):
        part = dot_nt(cotv[0], w[j].reshape(F, COLS))
        bp[lax.rem(j, 2) * 4 + j // 2] = part.astype(BF)
        return carry

    lax.fori_loop(0, 8, back, 0)
    b_core = send(bp.at[pl.ds((1 - pc) * 4, 4)], bcore, bcs.at[0], bcr.at[0], other)
    b_core.start()

    relay(xq, xq_y, xq_core, qcs, qcr)

    for c in tok_core:
        c.wait_recv()

    def hidden_tile(start, width):
        lhs = jnp.concatenate([xf[j, q] for j in range(8) for q in range(4)], axis=1)
        rhs = w[:, :, :, pl.ds(start, width)].reshape(4096, width)
        hid[:, pl.ds(start, width)] = dot(lhs, rhs).astype(BF)

    def hidden_step(n, carry):
        hidden_tile(pl.multiple_of(n * 256, 256), 256)
        return carry

    lax.fori_loop(0, 8, hidden_step, 0)
    hidden_tile(2048, 128)

    cx[0].wait_recv()
    fwd = [send(cotv.at[3, top], cotv.at[2, top], xs.at[4], xr.at[4], at_x(1))]
    fwd[0].start()
    cx[1].wait_recv()
    fwd.append(send(cotv.at[1, bot], cotv.at[2, bot], xs.at[5], xr.at[5], at_x(3)))
    fwd[1].start()

    b_core.wait_recv()
    b_y = []
    for d in (1, 2, 3):
        to = lax.rem(py + d, NY)
        total = bp[pc * 4 + to].astype(F32) + bcore[to].astype(F32)
        bp[pc * 4 + to] = total.astype(BF)
        c = send(bp.at[pc * 4 + to], by.at[d - 1], bys.at[d - 1], byr.at[d - 1], at_y(d))
        c.start()
        b_y.append(c)

    for c in xq_core:
        c.wait_recv()

    def put_square(j, rel, slab):
        at = REL_ORDER.index(rel)
        v = slab.astype(F32)
        v = (v * v).T.astype(BF)
        x2t[:, j, :, pl.ds(at * T, T)] = v.reshape(NZ, 16, T)

    def squares(j, carry):
        put_square(j, 0, xf[j, px])
        for d in (1, 2, 3):
            put_square(j, d, xq[j, d - 1])
        return carry

    lax.fori_loop(0, 8, squares, 0)

    cx[2].wait_recv()
    cx[3].wait_recv()

    def outer_tile(start, width):
        lhs = x2t[:, :, :, pl.ds(0, 3 * T)].reshape(1024, 3 * T)
        rhs = jnp.concatenate([square(cotv[r, :, pl.ds(start, width)]) for r in REL_ORDER[:3]], axis=0)
        acc[:, :, pl.ds(start, width)] = dot(lhs, rhs).reshape(NZ, 128, width)

    def outer_step(n, carry):
        outer_tile(pl.multiple_of(n * 256, 256), 256)
        return carry

    lax.fori_loop(0, 8, outer_step, 0)
    outer_tile(2048, 128)

    for c in fwd:
        c.wait_recv()

    def outer_last(start, width):
        lhs = x2t[:, :, :, pl.ds(3 * T, T)].reshape(1024, T)
        rhs = square(cotv[2, :, pl.ds(start, width)])
        acc[:, :, pl.ds(start, width)] += dot(lhs, rhs).reshape(NZ, 128, width)

    def outer_last_step(n, carry):
        outer_last(pl.multiple_of(n * 256, 256), 256)
        return carry

    lax.fori_loop(0, 8, outer_last_step, 0)
    outer_last(2048, 128)

    def chunks(da, db):
        for side, d in enumerate((da, db)):
            at = lax.rem(pz + d, NZ)

            def rearrange(pair, carry):
                o = acc[at, :, pl.ds(pl.multiple_of(pair * 128, 128), 128)].reshape(8, 2, 8, 128)
                p0 = o[:, 0].reshape(64, 128)
                p1 = o[:, 1].reshape(64, 128)
                a = jnp.where(low, p0, pltpu.roll(p1, 64, 1))
                b = jnp.where(low, pltpu.roll(p0, 64, 1), p1)
                gbuf[pair * 2, :, side * 128 : side * 128 + 128] = a.astype(BF)
                gbuf[pair * 2 + 1, :, side * 128 : side * 128 + 128] = b.astype(BF)
                return carry

            lax.fori_loop(0, PAIRS, rearrange, 0)

        def window(i, carry):
            rhs = jnp.concatenate([gbuf[group_slot[i * 4 + g]] for g in range(4)], axis=0)
            rows = pl.ds(pl.multiple_of(i * 64, 64), 64)
            out = dot(pick[rows, :], rhs).astype(BF)
            y[da, rows, :] = out[:, :128]
            y[db, rows, :] = out[:, 128:]
            return carry

        lax.fori_loop(0, 14, window, 0)

    rows_of = (pl.ds(0, HALF), pl.ds(HALF, HALF))

    def z_send(up, step, h):
        d = 4 - step if up else 4 + step
        buf, ssem, rsem, to = (rp, zps, zpr, at_z(1)) if up else (rm, zms, zmr, at_z(7))
        at = step * 2 + h
        return send(y.at[d, rows_of[h]], buf.at[step, rows_of[h]], ssem.at[at], rsem.at[at], to)

    sent = {}

    def z_step(up, step, h, add):
        if add:
            sent[(up, step - 1, h)].wait_recv()
            d = 4 - step if up else 4 + step
            buf = rp if up else rm
            y[d, rows_of[h], :] = (
                y[d, rows_of[h], :].astype(F32) + buf[step - 1, rows_of[h], :].astype(F32)
            ).astype(BF)
        c = z_send(up, step, h)
        c.start()
        sent[(up, step, h)] = c

    chunks(4, 3)
    z_step(True, 0, 0, False)
    z_step(False, 0, 1, False)
    z_step(True, 1, 1, False)
    chunks(5, 2)
    z_step(False, 1, 0, False)
    z_step(True, 1, 0, True)
    z_step(False, 1, 1, True)
    z_step(True, 2, 1, True)
    chunks(6, 1)
    z_step(False, 2, 0, True)
    chunks(7, 0)
    z_step(True, 2, 0, True)
    z_step(False, 2, 1, True)
    z_step(True, 3, 1, True)
    z_step(False, 3, 0, True)
    z_step(True, 3, 0, True)
    z_step(False, 3, 1, True)

    total = bp[pc * 4 + py].astype(F32) + bcore[py].astype(F32)
    for d in (1, 2, 3):
        b_y[d - 1].wait_recv()
        total = total + by[d - 1].astype(F32)
    grads[...] = dot_nt(total.astype(BF), perm).astype(BF)

    for h in range(2):
        sent[(True, 3, h)].wait_recv()
        sent[(False, 3, h)].wait_recv()
        value = (
            y[0, rows_of[h], :].astype(F32)
            + rp[3, rows_of[h], :].astype(F32)
            + rm[3, rows_of[h], :].astype(F32)
        )
        curv[rows_of[h], :] = value * (1.0 / 8192.0)

    for c in a2a + tok_y + tok_core + cx + xq_y + xq_core + fwd + [b_core] + b_y + list(sent.values()):
        c.wait_send()


def place_kernel(a, b, c, oa, ob, oc):
    oa[...] = a[...]
    ob[...] = b[...]
    oc[...] = c[...]


def tables(block_rows, block_slots):
    slot = jnp.arange(SLOTS * 64, dtype=jnp.int32)[:, None] // 64
    key = jnp.arange(SLOTS * 64, dtype=jnp.int32)[:, None]
    block = jnp.arange(KEPT, dtype=jnp.int32)[None, :]
    hit = (block_slots * 64 + block_rows)[None, :] == key
    before = (block_slots[None, :] < slot).astype(jnp.int32)
    offset = jnp.sum(jnp.where(hit, block + 65536, 0) - before, axis=1) - 65536
    lane = jnp.arange(256, dtype=jnp.int32)[None, :]
    here = (jnp.arange(SLOTS * 64, dtype=jnp.int32) // 64) % 4 * 64 + offset
    onehot = ((offset >= 0)[:, None] & (lane == here[:, None])).astype(BF)
    first = jnp.sum((block_slots[None, :] < jnp.arange(SLOTS, dtype=jnp.int32)[:, None]).astype(jnp.int32), axis=1)
    slot_group = first // 16
    place = (jnp.arange(KEPT, dtype=jnp.int32) // 16) % 4 * 64 + block_rows
    pick = (lane == place[:, None]).astype(BF)
    group_slot = block_slots[::16]
    return onehot, pick, slot_group, group_slot


def body(tokens, cotangent, weight_blocks, block_rows, block_slots):
    onehot, pick, slot_group, group_slot = tables(block_rows, block_slots)
    vm = pl.BlockSpec(memory_space=pltpu.VMEM)
    sm = pl.BlockSpec(memory_space=pltpu.SMEM)
    hb = pl.BlockSpec(memory_space=pl.ANY)
    sem = pltpu.SemaphoreType.DMA
    call = pl.pallas_call(
        kernel,
        out_shape=(
            jax.ShapeDtypeStruct((T, COLS), BF),
            jax.ShapeDtypeStruct((T, F), BF),
            jax.ShapeDtypeStruct((KEPT, 128), F32),
        ),
        in_specs=[vm, hb, hb, vm, vm, sm, sm],
        out_specs=(vm, vm, vm),
        scratch_shapes=[
            pltpu.VMEM((GROUPS + 4, 16, 512), BF),
            pltpu.VMEM((GROUPS + 4, 16, 512), BF),
            pltpu.VMEM((8, 32, 16, COLS), BF),
            pltpu.VMEM((4, T, COLS), BF),
            pltpu.VMEM((8, 4, T, 128), BF),
            pltpu.VMEM((8, 3, T, 128), BF),
            pltpu.VMEM((NZ, 8, 16, 4 * T), BF),
            pltpu.VMEM((NZ, 128, COLS), F32),
            pltpu.VMEM((SLOTS, 64, 256), BF),
            pltpu.VMEM((8, KEPT, 128), BF),
            pltpu.VMEM((4, KEPT, 128), BF),
            pltpu.VMEM((4, KEPT, 128), BF),
            pltpu.VMEM((8, T, F), BF),
            pltpu.VMEM((4, T, F), BF),
            pltpu.VMEM((3, T, F), BF),
            sem((3,)),
            sem((6,)), sem((6,)),
            sem((3,)), sem((3,)),
            sem((3,)), sem((3,)),
            sem((4,)), sem((4,)),
            sem((3,)), sem((3,)),
            sem((4,)), sem((4,)),
            sem((1,)), sem((1,)),
            sem((3,)), sem((3,)),
            sem((8,)), sem((8,)),
            sem((8,)), sem((8,)),
        ],
        compiler_params=pltpu.CompilerParams(
            collective_id=0, has_side_effects=True, vmem_limit_bytes=62 * 2**20
        ),
        cost_estimate=pl.CostEstimate(flops=14_000_000_000, bytes_accessed=12_000_000, transcendentals=0),
    )
    outs = call(tokens, cotangent, weight_blocks.reshape(GROUPS, 16, 4096), onehot, pick, slot_group, group_slot)
    place = pl.pallas_call(
        place_kernel,
        out_shape=[jax.ShapeDtypeStruct(o.shape, o.dtype) for o in outs],
        in_specs=[vm] * 3,
        out_specs=[vm] * 3,
    )
    return tuple(place(*outs))


def solution(mesh):
    placed = (P("dp", "tensor"), P("dp", "tensor"), P("tensor", None), P("tensor"), P("tensor"))
    return jax.shard_map(
        body,
        mesh=mesh,
        in_specs=placed,
        out_specs=(P("dp", "tensor"), P("dp", "tensor"), P("tensor", "dp")),
        check_vma=False,
    )
```

```python
import functools

import jax
import jax.numpy as jnp
from jax import lax
from jax.experimental import pallas as pl
from jax.experimental.pallas import tpu as pltpu
from jax.sharding import PartitionSpec as P

MESH = pl.DeviceIdType.MESH
BF = jnp.bfloat16
F32 = jnp.float32

NX, NZ, NY = 4, 8, 4
T = 256
F = 512
SLOTS = 34
PAIRS = 17
COLS = 2176
KEPT = 896
GROUPS = 56
QUARTER = KEPT // 4
REL_ORDER = (0, 1, 3, 2)


def dot(a, b):
    return jnp.dot(a, b, preferred_element_type=F32)


def dot_nt(a, b):
    return lax.dot_general(a, b, (((1,), (1,)), ((), ())), preferred_element_type=F32)


def square(v):
    w = v.astype(F32)
    return (w * w).astype(BF)


def kernel(
    tok, cot_hbm, wb_hbm, windows, slots,
    hid, grads, curv,
    slot_first, pick, onehot, wb0, wb1, w, cotv, xf, xq, x2t, acc, gbuf, y, rp, rm, bp, bcore, by,
    loc_sem, xs, xr, a_s, ar, ts, tr, tcs, tcr, qs, qr, qcs, qcr, bcs, bcr, bys, byr, zps, zpr, zms, zmr,
):
    dp = lax.axis_index("dp")
    te = lax.axis_index("tensor")
    px = dp // NZ
    pz = lax.rem(dp, NZ)
    py = te // 2
    pc = lax.rem(te, 2)

    def at_x(d):
        return (lax.rem(px + d, NX) * NZ + pz, te)

    def at_z(d):
        return (px * NZ + lax.rem(pz + d, NZ), te)

    def at_y(d):
        return (dp, lax.rem(py + d, NY) * 2 + pc)

    other = (dp, py * 2 + (1 - pc))

    def send(src, dst, ssem, rsem, where):
        return pltpu.make_async_remote_copy(
            src_ref=src, dst_ref=dst, send_sem=ssem, recv_sem=rsem,
            device_id=where, device_id_type=MESH,
        )

    load_cot = pltpu.make_async_copy(cot_hbm, cotv.at[0], loc_sem.at[0])
    load_cot.start()

    def load_wb(kk, slot):
        return pltpu.make_async_copy(
            wb_hbm.at[:, :, pl.ds(pl.multiple_of(kk * 512, 512), 512)],
            (wb0, wb1)[slot].at[pl.ds(0, GROUPS)],
            loc_sem.at[1 + slot],
        )

    load_wb(0, 0).start()
    load_wb(1, 1).start()

    barrier = pltpu.get_barrier_semaphore()
    peers = [at_x(1), at_x(2), at_x(3), at_y(1), at_y(2), at_y(3), other, at_z(1), at_z(7)]
    for who in peers:
        pl.semaphore_signal(barrier, inc=1, device_id=who, device_id_type=MESH)

    fi = lax.broadcasted_iota(jnp.int32, (F, F), 0)
    ci = lax.broadcasted_iota(jnp.int32, (F, F), 1)
    perm = ((fi // 64 == ci % 8) & (fi % 64 == ci // 8)).astype(F32).astype(BF)
    xp = dot(tok[...], perm).astype(BF)
    for q in range(4):
        xf[te, q] = xp[:, q * 128 : (q + 1) * 128]
    wb0[GROUPS:, :, :] = jnp.zeros((4, 16, 512), BF)
    wb1[GROUPS:, :, :] = jnp.zeros((4, 16, 512), BF)

    lane = lax.broadcasted_iota(jnp.int32, (1, 128), 1)

    def slot_step(s, at):
        slot_first[s] = at
        here = slots[jnp.minimum(at, GROUPS - 1) * 16]
        there = slots[jnp.minimum(at + 1, GROUPS - 1) * 16]
        one = (at < GROUPS) & (here == s)
        three = (at + 1 < GROUPS) & (there == s)
        return at + jnp.where(one, jnp.where(three, 3, 1), 0)

    lax.fori_loop(0, SLOTS, slot_step, jnp.int32(0))

    def pick_step(v, carry):
        k = jnp.where(lane < 64, windows[pl.ds(v * 8, 1), :], windows[pl.ds(v * 8 + 4, 1), :])
        wanted = lax.rem(lane, 64) // 16 * 64 + lax.rem(k, 64)
        e = (lax.broadcasted_iota(jnp.int32, (256, 128), 0) == wanted).astype(F32)
        pick[pl.ds(pl.multiple_of(v * 128, 128), 128), :] = e.T.astype(BF)
        return carry

    def place_rows(q, ns):
        parts = []
        for i in range(0, ns, 2):
            s = q * 4 + i
            k0 = windows[pl.ds(slot_first[s], 1), :] - s * 64
            k1 = windows[pl.ds(slot_first[s + 1], 1), :] - (s * 64 + 64)
            k = jnp.where(lane < 64, k0, k1)
            base = jnp.where(lane < 64, i * 64, i * 64 + 64)
            parts.append(jnp.where((k >= 0) & (k < 64), k + base, -1))
        wanted = jnp.concatenate(parts, axis=1) if len(parts) > 1 else parts[0]
        n = ns * 64
        e = (lax.broadcasted_iota(jnp.int32, (n, n), 0) == wanted).astype(F32).astype(BF)
        onehot[pl.ds(pl.multiple_of(q * 256, 256), n), pl.ds(0, n)] = e

    def place_step(q, carry):
        place_rows(q, 4)
        return carry

    lax.fori_loop(0, 8, place_step, 0)
    place_rows(8, 2)

    pl.semaphore_wait(barrier, len(peers))

    a2a = []
    for d in (1, 2, 3):
        a2a.append(send(xf.at[te, lax.rem(px + d, NX)], xq.at[te, 3 - d], a_s.at[3 - d], ar.at[3 - d], at_x(d)))
    for c in a2a:
        c.start()
    tok_y = [send(xf.at[te], xf.at[te], ts.at[d - 1], tr.at[d - 1], at_y(d)) for d in (1, 2, 3)]
    for c in tok_y:
        c.start()
    tok_core = [send(xf.at[te], xf.at[te], tcs.at[0], tcr.at[0], other)]
    tok_core[0].start()

    load_cot.wait()
    parts = [pl.ds(i * 64, 64) for i in range(4)]
    cx = []

    def send_part(i):
        at = len(cx)
        cx.append(send(cotv.at[0, parts[i]], cotv.at[3, parts[i]], xs.at[at], xr.at[at], at_x(1)))
        cx[-1].start()
        at += 1
        cx.append(send(cotv.at[0, parts[3 - i]], cotv.at[1, parts[3 - i]], xs.at[at], xr.at[at], at_x(3)))
        cx[-1].start()

    send_part(0)
    send_part(1)

    low = lax.broadcasted_iota(jnp.int32, (64, 128), 1) < 64

    def expand_group(q, ns, kk, slot):
        lhs = onehot[pl.ds(pl.multiple_of(q * 256, 256), ns * 64), pl.ds(0, ns * 64)]
        buf = (wb0, wb1)[slot]
        firsts = [slot_first[q * 4 + i] for i in range(ns)]
        for side in range(2):
            rhs = jnp.concatenate(
                [buf[pl.ds(first, 4), :, pl.ds(side * 256, 256)].reshape(64, 256) for first in firsts], axis=0
            )
            out = dot(lhs, rhs)
            for pair in range(ns // 2):
                for k2 in range(2):
                    a = out[pair * 128 : pair * 128 + 64, k2 * 128 : k2 * 128 + 128]
                    b = out[pair * 128 + 64 : pair * 128 + 128, k2 * 128 : k2 * 128 + 128]
                    p0 = jnp.where(low, a, pltpu.roll(b, 64, 1)).reshape(8, 1, 8, 128)
                    p1 = jnp.where(low, pltpu.roll(a, 64, 1), b).reshape(8, 1, 8, 128)
                    tile = jnp.concatenate([p0, p1], axis=1).reshape(8, 16, 128).astype(BF)
                    w[:, kk * 4 + side * 2 + k2, :, pl.ds(pl.multiple_of(q * 256 + pair * 128, 128), 128)] = tile

    def expand_step(kk, slot):
        load_wb(kk, slot).wait()

        def group(q, carry):
            expand_group(q, 4, kk, slot)
            return carry

        lax.fori_loop(0, 8, group, 0, unroll=2)
        expand_group(8, 2, kk, slot)

    def expand_two(i, carry):
        for slot in range(2):
            expand_step(i * 2 + slot, slot)
            load_wb(i * 2 + 2 + slot, slot).start()
        return carry

    lax.fori_loop(0, 2, expand_two, 0)

    cx[0].wait_send()
    cx[1].wait_send()
    send_part(2)

    for c in a2a:
        c.wait_recv()
    xq_y = [send(xq.at[te], xq.at[te], qs.at[d - 1], qr.at[d - 1], at_y(d)) for d in (1, 2, 3)]
    for c in xq_y:
        c.start()
    xq_core = [send(xq.at[te], xq.at[te], qcs.at[0], qcr.at[0], other)]
    xq_core[0].start()

    lax.fori_loop(2, 3, expand_two, 0)
    for slot in range(2):
        expand_step(6 + slot, slot)

    def relay(buf, copies, core, ssem, rsem):
        for d in (1, 2, 3):
            copies[d - 1].wait_recv()
            src = lax.rem(py + NY - d, NY) * 2 + pc
            c = send(buf.at[src], buf.at[src], ssem.at[d], rsem.at[d], other)
            c.start()
            core.append(c)

    cx[2].wait_send()
    cx[3].wait_send()
    send_part(3)

    relay(xf, tok_y, tok_core, tcs, tcr)

    def back(j, carry):
        part = dot_nt(w[pl.ds(j * 2, 2)].reshape(2 * F, COLS), cotv[0]).astype(BF)
        bp[j] = part[:F]
        bp[4 + j] = part[F:]
        return carry

    lax.fori_loop(0, 4, back, 0)
    b_core = send(bp.at[pl.ds((1 - pc) * 4, 4)], bcore, bcs.at[0], bcr.at[0], other)
    b_core.start()

    fwd = []
    for i in (0, 1):
        cx[2 * i].wait_recv()
        fwd.append(send(cotv.at[3, parts[i]], cotv.at[2, parts[i]], xs.at[8 + 2 * i], xr.at[8 + 2 * i], at_x(1)))
        fwd[-1].start()
        cx[2 * i + 1].wait_recv()
        fwd.append(
            send(cotv.at[1, parts[3 - i]], cotv.at[2, parts[3 - i]], xs.at[9 + 2 * i], xr.at[9 + 2 * i], at_x(3))
        )
        fwd[-1].start()

    relay(xq, xq_y, xq_core, qcs, qcr)

    for c in tok_core:
        c.wait_recv()

    def hidden_tile(start, width):
        lhs = jnp.concatenate([xf[j, q] for j in range(8) for q in range(4)], axis=1)
        rhs = w[:, :, :, pl.ds(start, width)].reshape(4096, width)
        hid[:, pl.ds(start, width)] = dot(lhs, rhs).astype(BF)

    def hidden_step(n, carry):
        hidden_tile(pl.multiple_of(n * 256, 256), 256)
        return carry

    lax.fori_loop(0, 8, hidden_step, 0)
    lax.fori_loop(0, 7, pick_step, 0)
    hidden_tile(2048, 128)

    b_core.wait_recv()
    b_y = []
    for d in (1, 2, 3):
        to = lax.rem(py + d, NY)
        total = bp[pc * 4 + to].astype(F32) + bcore[to].astype(F32)
        bp[pc * 4 + to] = total.astype(BF)
        c = send(bp.at[pc * 4 + to], by.at[d - 1], bys.at[d - 1], byr.at[d - 1], at_y(d))
        c.start()
        b_y.append(c)

    for c in xq_core:
        c.wait_recv()

    def put_square(j, rel, slab):
        at = REL_ORDER.index(rel)
        v = slab.astype(F32)
        v = (v * v).T.astype(BF)
        x2t[:, j, :, pl.ds(at * T, T)] = v.reshape(NZ, 16, T)

    def squares(j, carry):
        put_square(j, 0, xf[j, px])
        for d in (1, 2, 3):
            put_square(j, d, xq[j, d - 1])
        return carry

    lax.fori_loop(0, 8, squares, 0)

    for c in cx[4:]:
        c.wait_recv()

    def outer_tile(start, width):
        lhs = x2t[:, :, :, pl.ds(0, 3 * T)].reshape(1024, 3 * T)
        rhs = jnp.concatenate([square(cotv[r, :, pl.ds(start, width)]) for r in REL_ORDER[:3]], axis=0)
        acc[:, :, pl.ds(start, width)] = dot(lhs, rhs).reshape(NZ, 128, width)

    def outer_step(n, carry):
        outer_tile(pl.multiple_of(n * 256, 256), 256)
        return carry

    lax.fori_loop(0, 8, outer_step, 0)
    outer_tile(2048, 128)

    for c in fwd:
        c.wait_recv()

    def square_last(i, carry):
        rows = pl.ds(pl.multiple_of(i * 64, 64), 64)
        cotv[2, rows, :] = square(cotv[2, rows, :])
        return carry

    lax.fori_loop(0, 4, square_last, 0)

    def chunks(da, db):
        at = [lax.rem(pz + d, NZ) for d in (da, db)]

        def rearrange(start, width):
            lhs = jnp.concatenate([x2t[z, :, :, pl.ds(3 * T, T)].reshape(128, T) for z in at], axis=0)
            last = dot(lhs, cotv[2, :, pl.ds(start, width)])
            for side in range(2):
                whole = acc[at[side], :, pl.ds(start, width)] + last[side * 128 : side * 128 + 128]
                for pair in range(width // 128):
                    o = whole[:, pair * 128 : pair * 128 + 128].reshape(8, 2, 8, 128)
                    p0 = o[:, 0].reshape(64, 128)
                    p1 = o[:, 1].reshape(64, 128)
                    a = jnp.where(low, p0, pltpu.roll(p1, 64, 1))
                    b = jnp.where(low, pltpu.roll(p0, 64, 1), p1)
                    slot = start // 64 + pair * 2
                    gbuf[slot, :, side * 128 : side * 128 + 128] = a.astype(BF)
                    gbuf[slot + 1, :, side * 128 : side * 128 + 128] = b.astype(BF)

        def rearrange_step(n, carry):
            rearrange(pl.multiple_of(n * 256, 256), 256)
            return carry

        lax.fori_loop(0, 8, rearrange_step, 0, unroll=2)
        rearrange(2048, 128)

        def window(i, carry):
            rhs = jnp.concatenate([gbuf[slots[(i * 4 + g) * 16]] for g in range(4)], axis=0)
            rows = pl.ds(pl.multiple_of(i * 64, 64), 64)
            out = dot(pick[rows, :], rhs).astype(BF)
            y[da, rows, :] = out[:, :128]
            y[db, rows, :] = out[:, 128:]
            return carry

        lax.fori_loop(0, 14, window, 0, unroll=7)

    rows_of = [pl.ds(i * QUARTER, QUARTER) for i in range(4)]
    sent = {}

    def z_step(up, step, h):
        d = 4 - step if up else 4 + step
        buf, ssem, rsem, to = (rp, zps, zpr, at_z(1)) if up else (rm, zms, zmr, at_z(7))
        rows = rows_of[h]
        if (up, step - 1, h) in sent:
            sent[(up, step - 1, h)].wait_recv()
            y[d, rows, :] = (y[d, rows, :].astype(F32) + buf[step - 1, rows, :].astype(F32)).astype(BF)
        at = step * 4 + h
        c = send(y.at[d, rows], buf.at[step, rows], ssem.at[at], rsem.at[at], to)
        c.start()
        sent[(up, step, h)] = c

    def z_steps(up, step, parts_of):
        for h in parts_of:
            z_step(up, step, h)

    chunks(4, 3)
    z_steps(True, 0, (0, 1))
    z_steps(False, 0, (3, 2))
    z_steps(True, 1, (2, 3))
    chunks(5, 2)
    z_steps(False, 1, (1, 0))
    z_steps(True, 1, (0, 1))
    z_steps(False, 1, (3, 2))
    chunks(6, 1)
    z_steps(True, 2, (2, 3))
    z_steps(False, 2, (1, 0))
    z_steps(True, 2, (0, 1))
    z_steps(False, 2, (3, 2))
    chunks(7, 0)
    z_steps(True, 3, (2, 3))
    z_steps(False, 3, (1, 0))
    z_steps(True, 3, (0, 1))
    z_steps(False, 3, (3, 2))

    total = bp[pc * 4 + py].astype(F32) + bcore[py].astype(F32)
    for d in (1, 2, 3):
        b_y[d - 1].wait_recv()
        total = total + by[d - 1].astype(F32)
    grads[...] = dot(perm, total.astype(BF)).T.astype(BF)

    for h in (2, 1, 0, 3):
        sent[(True, 3, h)].wait_recv()
        sent[(False, 3, h)].wait_recv()
        value = (
            y[0, rows_of[h], :].astype(F32)
            + rp[3, rows_of[h], :].astype(F32)
            + rm[3, rows_of[h], :].astype(F32)
        )
        curv[rows_of[h], :] = value * (1.0 / 8192.0)

    for c in a2a + tok_y + tok_core + cx[4:] + xq_y + xq_core + fwd + [b_core] + b_y + list(sent.values()):
        c.wait_send()


def place_kernel(a, b, c, oa, ob, oc):
    oa[...] = a[...]
    ob[...] = b[...]
    oc[...] = c[...]


def tables(block_rows, block_slots):
    keys = jnp.pad(block_slots * 64 + block_rows, (0, 128), constant_values=-1).reshape(64, 16)
    window = jnp.concatenate([keys[i : i + 60] for i in range(4)] * 2, axis=1)
    return window


def body(tokens, cotangent, weight_blocks, block_rows, block_slots):
    window = tables(block_rows, block_slots)
    vm = pl.BlockSpec(memory_space=pltpu.VMEM)
    sm = pl.BlockSpec(memory_space=pltpu.SMEM)
    hb = pl.BlockSpec(memory_space=pl.ANY)
    sem = pltpu.SemaphoreType.DMA
    call = pl.pallas_call(
        kernel,
        out_shape=(
            jax.ShapeDtypeStruct((T, COLS), BF),
            jax.ShapeDtypeStruct((T, F), BF),
            jax.ShapeDtypeStruct((KEPT, 128), F32),
        ),
        in_specs=[vm, hb, hb, vm, sm],
        out_specs=(vm, vm, vm),
        scratch_shapes=[
            pltpu.SMEM((SLOTS,), jnp.int32),
            pltpu.VMEM((KEPT, 256), BF),
            pltpu.VMEM((SLOTS * 64, 256), BF),
            pltpu.VMEM((GROUPS + 4, 16, 512), BF),
            pltpu.VMEM((GROUPS + 4, 16, 512), BF),
            pltpu.VMEM((8, 32, 16, COLS), BF),
            pltpu.VMEM((4, T, COLS), BF),
            pltpu.VMEM((8, 4, T, 128), BF),
            pltpu.VMEM((8, 3, T, 128), BF),
            pltpu.VMEM((NZ, 8, 16, 4 * T), BF),
            pltpu.VMEM((NZ, 128, COLS), F32),
            pltpu.VMEM((SLOTS, 64, 256), BF),
            pltpu.VMEM((8, KEPT, 128), BF),
            pltpu.VMEM((4, KEPT, 128), BF),
            pltpu.VMEM((4, KEPT, 128), BF),
            pltpu.VMEM((8, F, T), BF),
            pltpu.VMEM((4, F, T), BF),
            pltpu.VMEM((3, F, T), BF),
            sem((3,)),
            sem((12,)), sem((12,)),
            sem((3,)), sem((3,)),
            sem((3,)), sem((3,)),
            sem((4,)), sem((4,)),
            sem((3,)), sem((3,)),
            sem((4,)), sem((4,)),
            sem((1,)), sem((1,)),
            sem((3,)), sem((3,)),
            sem((16,)), sem((16,)),
            sem((16,)), sem((16,)),
        ],
        compiler_params=pltpu.CompilerParams(
            collective_id=0, has_side_effects=True, vmem_limit_bytes=62 * 2**20
        ),
        cost_estimate=pl.CostEstimate(flops=14_000_000_000, bytes_accessed=12_000_000, transcendentals=0),
    )
    outs = call(tokens, cotangent, weight_blocks.reshape(GROUPS, 16, 4096), window, block_slots)
    place = pl.pallas_call(
        place_kernel,
        out_shape=[jax.ShapeDtypeStruct(o.shape, o.dtype) for o in outs],
        in_specs=[vm] * 3,
        out_specs=[vm] * 3,
    )
    return tuple(place(*outs))


def solution(mesh):
    placed = (P("dp", "tensor"), P("dp", "tensor"), P("tensor", None), P("tensor"), P("tensor"))
    return jax.shard_map(
        body,
        mesh=mesh,
        in_specs=placed,
        out_specs=(P("dp", "tensor"), P("dp", "tensor"), P("tensor", "dp")),
        check_vma=False,
    )
```

```python
import functools

import jax
import jax.numpy as jnp
from jax import lax
from jax.experimental import pallas as pl
from jax.experimental.pallas import tpu as pltpu
from jax.sharding import PartitionSpec as P

MESH = pl.DeviceIdType.MESH
BF = jnp.bfloat16
F32 = jnp.float32

NX, NZ, NY = 4, 8, 4
T = 256
F = 512
SLOTS = 34
PAIRS = 17
COLS = 2176
KEPT = 896
GROUPS = 56
QUARTER = KEPT // 4
EARLY = 1664
REL_ORDER = (0, 1, 3, 2)


def dot(a, b):
    return jnp.dot(a, b, preferred_element_type=F32)


def dot_nt(a, b):
    return lax.dot_general(a, b, (((1,), (1,)), ((), ())), preferred_element_type=F32)


def square(v):
    w = v.astype(F32)
    return (w * w).astype(BF)


def kernel(
    tok, cot_hbm, wb_hbm, windows, slots,
    hid_out, grads_out, curv,
    hid, grads, slot_first, pick, onehot, wb0, wb1, w, cotv, xf, xq, x2t, acc, gbuf, y, rp, rm, bp, bcore, by,
    loc_sem, xs, xr, a_s, ar, ts, tr, tcs, tcr, qs, qr, qcs, qcr, bcs, bcr, bys, byr, zps, zpr, zms, zmr,
):
    dp = lax.axis_index("dp")
    te = lax.axis_index("tensor")
    px = dp // NZ
    pz = lax.rem(dp, NZ)
    py = te // 2
    pc = lax.rem(te, 2)

    def at_x(d):
        return (lax.rem(px + d, NX) * NZ + pz, te)

    def at_z(d):
        return (px * NZ + lax.rem(pz + d, NZ), te)

    def at_y(d):
        return (dp, lax.rem(py + d, NY) * 2 + pc)

    other = (dp, py * 2 + (1 - pc))

    def send(src, dst, ssem, rsem, where):
        return pltpu.make_async_remote_copy(
            src_ref=src, dst_ref=dst, send_sem=ssem, recv_sem=rsem,
            device_id=where, device_id_type=MESH,
        )

    load_cot = pltpu.make_async_copy(cot_hbm, cotv.at[0], loc_sem.at[0])
    load_cot.start()

    def load_wb(kk, slot):
        return pltpu.make_async_copy(
            wb_hbm.at[:, :, pl.ds(pl.multiple_of(kk * 512, 512), 512)],
            (wb0, wb1)[slot].at[pl.ds(0, GROUPS)],
            loc_sem.at[1 + slot],
        )

    load_wb(0, 0).start()
    load_wb(1, 1).start()

    barrier = pltpu.get_barrier_semaphore()
    peers = [at_x(1), at_x(2), at_x(3), at_y(1), at_y(2), at_y(3), other, at_z(1), at_z(7)]
    for who in peers:
        pl.semaphore_signal(barrier, inc=1, device_id=who, device_id_type=MESH)

    fi = lax.broadcasted_iota(jnp.int32, (F, F), 0)
    ci = lax.broadcasted_iota(jnp.int32, (F, F), 1)
    perm = ((fi // 64 == ci % 8) & (fi % 64 == ci // 8)).astype(F32).astype(BF)
    xp = dot(tok[...], perm).astype(BF)
    for q in range(4):
        xf[te, q] = xp[:, q * 128 : (q + 1) * 128]
    wb0[GROUPS:, :, :] = jnp.zeros((4, 16, 512), BF)
    wb1[GROUPS:, :, :] = jnp.zeros((4, 16, 512), BF)

    pl.semaphore_wait(barrier, len(peers))

    a2a = []
    for d in (1, 2, 3):
        a2a.append(send(xf.at[te, lax.rem(px + d, NX)], xq.at[te, 3 - d], a_s.at[3 - d], ar.at[3 - d], at_x(d)))
    for c in a2a:
        c.start()
    tok_y = [send(xf.at[te], xf.at[te], ts.at[d - 1], tr.at[d - 1], at_y(d)) for d in (1, 2, 3)]
    for c in tok_y:
        c.start()
    tok_core = [send(xf.at[te], xf.at[te], tcs.at[0], tcr.at[0], other)]
    tok_core[0].start()

    load_cot.wait()
    parts = [pl.ds(i * 64, 64) for i in range(4)]
    cx = []

    def send_part(i):
        at = len(cx)
        cx.append(send(cotv.at[0, parts[i]], cotv.at[3, parts[i]], xs.at[at], xr.at[at], at_x(1)))
        cx[-1].start()
        at += 1
        cx.append(send(cotv.at[0, parts[3 - i]], cotv.at[1, parts[3 - i]], xs.at[at], xr.at[at], at_x(3)))
        cx[-1].start()

    send_part(0)
    send_part(1)

    lane = lax.broadcasted_iota(jnp.int32, (1, 128), 1)

    def slot_step(s, at):
        slot_first[s] = at
        here = slots[jnp.minimum(at, GROUPS - 1) * 16]
        there = slots[jnp.minimum(at + 1, GROUPS - 1) * 16]
        one = (at < GROUPS) & (here == s)
        three = (at + 1 < GROUPS) & (there == s)
        return at + jnp.where(one, jnp.where(three, 3, 1), 0)

    lax.fori_loop(0, SLOTS, slot_step, jnp.int32(0))

    def pick_step(v, carry):
        k = jnp.where(lane < 64, windows[pl.ds(v * 8, 1), :], windows[pl.ds(v * 8 + 4, 1), :])
        wanted = lax.rem(lane, 64) // 16 * 64 + lax.rem(k, 64)
        e = (lax.broadcasted_iota(jnp.int32, (256, 128), 0) == wanted).astype(F32)
        pick[pl.ds(pl.multiple_of(v * 128, 128), 128), :] = e.T.astype(BF)
        return carry

    def place_rows(q, ns):
        parts = []
        for i in range(0, ns, 2):
            s = q * 4 + i
            k0 = windows[pl.ds(slot_first[s], 1), :] - s * 64
            k1 = windows[pl.ds(slot_first[s + 1], 1), :] - (s * 64 + 64)
            k = jnp.where(lane < 64, k0, k1)
            base = jnp.where(lane < 64, i * 64, i * 64 + 64)
            parts.append(jnp.where((k >= 0) & (k < 64), k + base, -1))
        wanted = jnp.concatenate(parts, axis=1) if len(parts) > 1 else parts[0]
        n = ns * 64
        e = (lax.broadcasted_iota(jnp.int32, (n, n), 0) == wanted).astype(F32).astype(BF)
        onehot[pl.ds(pl.multiple_of(q * 256, 256), n), pl.ds(0, n)] = e

    def place_step(q, carry):
        place_rows(q, 4)
        return carry

    lax.fori_loop(0, 8, place_step, 0)
    place_rows(8, 2)

    low = lax.broadcasted_iota(jnp.int32, (64, 128), 1) < 64

    def expand_group(q, ns, kk, slot):
        lhs = onehot[pl.ds(pl.multiple_of(q * 256, 256), ns * 64), pl.ds(0, ns * 64)]
        buf = (wb0, wb1)[slot]
        firsts = [slot_first[q * 4 + i] for i in range(ns)]
        for side in range(2):
            rhs = jnp.concatenate(
                [buf[pl.ds(first, 4), :, pl.ds(side * 256, 256)].reshape(64, 256) for first in firsts], axis=0
            )
            out = dot(lhs, rhs)
            for pair in range(ns // 2):
                for k2 in range(2):
                    a = out[pair * 128 : pair * 128 + 64, k2 * 128 : k2 * 128 + 128]
                    b = out[pair * 128 + 64 : pair * 128 + 128, k2 * 128 : k2 * 128 + 128]
                    p0 = jnp.where(low, a, pltpu.roll(b, 64, 1)).reshape(8, 1, 8, 128)
                    p1 = jnp.where(low, pltpu.roll(a, 64, 1), b).reshape(8, 1, 8, 128)
                    tile = jnp.concatenate([p0, p1], axis=1).reshape(8, 16, 128).astype(BF)
                    w[:, kk * 4 + side * 2 + k2, :, pl.ds(pl.multiple_of(q * 256 + pair * 128, 128), 128)] = tile

    def expand_step(kk, slot):
        load_wb(kk, slot).wait()

        def group(q, carry):
            expand_group(q, 4, kk, slot)
            return carry

        lax.fori_loop(0, 8, group, 0, unroll=2)
        expand_group(8, 2, kk, slot)

    def expand_two(i, carry):
        for slot in range(2):
            expand_step(i * 2 + slot, slot)
            load_wb(i * 2 + 2 + slot, slot).start()
        return carry

    lax.fori_loop(0, 2, expand_two, 0)

    cx[0].wait_send()
    cx[1].wait_send()
    send_part(2)

    for c in a2a:
        c.wait_recv()
    xq_y = [send(xq.at[te], xq.at[te], qs.at[d - 1], qr.at[d - 1], at_y(d)) for d in (1, 2, 3)]
    for c in xq_y:
        c.start()
    xq_core = [send(xq.at[te], xq.at[te], qcs.at[0], qcr.at[0], other)]
    xq_core[0].start()

    lax.fori_loop(2, 3, expand_two, 0)
    for slot in range(2):
        expand_step(6 + slot, slot)

    def relay(buf, copies, core, ssem, rsem):
        for d in (1, 2, 3):
            copies[d - 1].wait_recv()
            src = lax.rem(py + NY - d, NY) * 2 + pc
            c = send(buf.at[src], buf.at[src], ssem.at[d], rsem.at[d], other)
            c.start()
            core.append(c)

    cx[2].wait_send()
    cx[3].wait_send()
    send_part(3)

    relay(xf, tok_y, tok_core, tcs, tcr)

    def back(j, carry):
        part = dot_nt(w[pl.ds(j * 2, 2)].reshape(2 * F, COLS), cotv[0]).astype(BF)
        bp[j] = part[:F]
        bp[4 + j] = part[F:]
        return carry

    lax.fori_loop(0, 4, back, 0)
    b_core = send(bp.at[pl.ds((1 - pc) * 4, 4)], bcore, bcs.at[0], bcr.at[0], other)
    b_core.start()

    for c in cx[:4]:
        c.wait_recv()
    fwd = []

    def forward(columns):
        for up in (True, False):
            rel, rows, to = (3, pl.ds(0, 128), at_x(1)) if up else (1, pl.ds(128, 128), at_x(3))
            at = 8 + len(fwd)
            fwd.append(send(cotv.at[rel, rows, columns], cotv.at[2, rows, columns], xs.at[at], xr.at[at], to))
            fwd[-1].start()

    forward(pl.ds(0, EARLY))

    relay(xq, xq_y, xq_core, qcs, qcr)

    for c in tok_core:
        c.wait_recv()

    def hidden_tile(start, width):
        lhs = jnp.concatenate([xf[j, q] for j in range(8) for q in range(4)], axis=1)
        rhs = w[:, :, :, pl.ds(start, width)].reshape(4096, width)
        hid[:, pl.ds(start, width)] = dot(lhs, rhs).astype(BF)

    def hidden_step(n, carry):
        hidden_tile(pl.multiple_of(n * 256, 256), 256)
        return carry

    lax.fori_loop(0, 4, hidden_step, 0)
    lax.fori_loop(0, 7, pick_step, 0)

    b_core.wait_recv()
    b_y = []
    for d in (1, 2, 3):
        to = lax.rem(py + d, NY)
        total = bp[pc * 4 + to].astype(F32) + bcore[to].astype(F32)
        bp[pc * 4 + to] = total.astype(BF)
        c = send(bp.at[pc * 4 + to], by.at[d - 1], bys.at[d - 1], byr.at[d - 1], at_y(d))
        c.start()
        b_y.append(c)

    for c in xq_core:
        c.wait_recv()

    def put_square(j, rel, slab):
        at = REL_ORDER.index(rel)
        v = slab.astype(F32)
        v = (v * v).T.astype(BF)
        x2t[:, j, :, pl.ds(at * T, T)] = v.reshape(NZ, 16, T)

    def squares(j, carry):
        put_square(j, 0, xf[j, px])
        for d in (1, 2, 3):
            put_square(j, d, xq[j, d - 1])
        return carry

    lax.fori_loop(0, 8, squares, 0)

    for c in cx[4:]:
        c.wait_recv()

    def outer_tile(start, width):
        lhs = x2t[:, :, :, pl.ds(0, 3 * T)].reshape(1024, 3 * T)
        rhs = jnp.concatenate([square(cotv[r, :, pl.ds(start, width)]) for r in REL_ORDER[:3]], axis=0)
        acc[:, :, pl.ds(start, width)] = dot(lhs, rhs).reshape(NZ, 128, width)

    def outer_step(n, carry):
        outer_tile(pl.multiple_of(n * 256, 256), 256)
        return carry

    lax.fori_loop(0, 8, outer_step, 0)
    outer_tile(2048, 128)

    for c in fwd[:2]:
        c.wait_send()
    forward(pl.ds(EARLY, COLS - EARLY))

    def square_last(start, width):
        def step(i, carry):
            at = (2, pl.ds(pl.multiple_of(i * 64, 64), 64), pl.ds(start, width))
            cotv[at] = square(cotv[at])
            return carry

        lax.fori_loop(0, 4, step, 0)

    def rearrange(g, da, db, start, width):
        at = [lax.rem(pz + d, NZ) for d in (da, db)]
        lhs = jnp.concatenate([x2t[z, :, :, pl.ds(3 * T, T)].reshape(128, T) for z in at], axis=0)
        last = dot(lhs, cotv[2, :, pl.ds(start, width)])
        for side in range(2):
            whole = acc[at[side], :, pl.ds(start, width)] + last[side * 128 : side * 128 + 128]
            for pair in range(width // 128):
                o = whole[:, pair * 128 : pair * 128 + 128].reshape(8, 2, 8, 128)
                p0 = o[:, 0].reshape(64, 128)
                p1 = o[:, 1].reshape(64, 128)
                a = jnp.where(low, p0, pltpu.roll(p1, 64, 1))
                b = jnp.where(low, pltpu.roll(p0, 64, 1), p1)
                slot = start // 64 + pair * 2
                gbuf[g, slot, :, side * 128 : side * 128 + 128] = a.astype(BF)
                gbuf[g, slot + 1, :, side * 128 : side * 128 + 128] = b.astype(BF)

    def chunks(g, da, db, columns, windows_of):
        def rearrange_step(n, carry):
            rearrange(g, da, db, pl.multiple_of(n * 256, 256), 256)
            return carry

        first, end = columns
        lax.fori_loop((first + 255) // 256, end // 256, rearrange_step, 0, unroll=2)
        if first % 256:
            rearrange(g, da, db, first, 128)
        if end % 256:
            rearrange(g, da, db, end - 128, 128)

        def window(i, carry):
            rhs = jnp.concatenate([gbuf[g, slots[(i * 4 + k) * 16]] for k in range(4)], axis=0)
            rows = pl.ds(pl.multiple_of(i * 64, 64), 64)
            out = dot(pick[rows, :], rhs).astype(BF)
            y[da, rows, :] = out[:, :128]
            y[db, rows, :] = out[:, 128:]
            return carry

        lax.fori_loop(*windows_of, window, 0, unroll=7)

    rows_of = [pl.ds(i * QUARTER, QUARTER) for i in range(4)]
    sent = {}

    def z_step(up, step, h):
        d = 4 - step if up else 4 + step
        buf, ssem, rsem, to = (rp, zps, zpr, at_z(1)) if up else (rm, zms, zmr, at_z(7))
        rows = rows_of[h]
        if (up, step - 1, h) in sent:
            sent[(up, step - 1, h)].wait_recv()
            y[d, rows, :] = (y[d, rows, :].astype(F32) + buf[step - 1, rows, :].astype(F32)).astype(BF)
        at = step * 4 + h
        c = send(y.at[d, rows], buf.at[step, rows], ssem.at[at], rsem.at[at], to)
        c.start()
        sent[(up, step, h)] = c

    def z_steps(up, step, parts_of):
        for h in parts_of:
            z_step(up, step, h)

    early, late, every = (0, EARLY), (EARLY, COLS), (0, COLS)
    half_a, half_b, both = (0, 7), (7, 14), (0, 14)
    for c in fwd[:2]:
        c.wait_recv()
    square_last(0, EARLY)
    chunks(0, 4, 3, early, half_a)
    z_step(True, 0, 0)
    z_step(False, 0, 1)
    z_step(True, 1, 1)
    chunks(1, 5, 2, early, half_a)
    z_step(False, 1, 0)
    for c in fwd[2:]:
        c.wait_recv()
    square_last(EARLY, COLS - EARLY)
    chunks(0, 4, 3, late, half_b)
    z_step(True, 0, 2)
    z_step(False, 0, 3)
    z_step(True, 1, 3)
    chunks(1, 5, 2, late, half_b)
    z_step(False, 1, 2)
    z_step(True, 1, 0)
    z_step(False, 1, 1)
    z_step(True, 1, 2)
    z_step(False, 1, 3)
    chunks(0, 6, 1, every, both)
    for h in (1, 0, 3, 2):
        z_step(True, 2, h)
        z_step(False, 2, h ^ 1)
    chunks(1, 7, 0, every, both)
    lax.fori_loop(4, 6, hidden_step, 0)
    for h in (1, 0, 3, 2):
        z_step(True, 3, h)
        z_step(False, 3, h ^ 1)
    lax.fori_loop(6, 8, hidden_step, 0)
    hidden_tile(2048, 128)
    store_hid = pltpu.make_async_copy(hid, hid_out, loc_sem.at[0])
    store_hid.start()

    total = bp[pc * 4 + py].astype(F32) + bcore[py].astype(F32)
    for d in (1, 2, 3):
        b_y[d - 1].wait_recv()
        total = total + by[d - 1].astype(F32)
    grads[...] = dot(perm, total.astype(BF)).T.astype(BF)
    store_grads = pltpu.make_async_copy(grads, grads_out, loc_sem.at[1])
    store_grads.start()

    for h in (1, 0, 3, 2):
        sent[(True, 3, h)].wait_recv()
        sent[(False, 3, h)].wait_recv()
        value = (
            y[0, rows_of[h], :].astype(F32)
            + rp[3, rows_of[h], :].astype(F32)
            + rm[3, rows_of[h], :].astype(F32)
        )
        curv[rows_of[h], :] = value * (1.0 / 8192.0)

    store_hid.wait()
    store_grads.wait()
    for c in a2a + tok_y + tok_core + cx[4:] + xq_y + xq_core + fwd[2:] + [b_core] + b_y + list(sent.values()):
        c.wait_send()


def place_kernel(a, b, c, oa, ob, oc, va, vb, vc, sem):
    pieces = []
    for src, mid, dst, cuts in ((a, va, oa, 4), (c, vc, oc, 2), (b, vb, ob, 1)):
        size = src.shape[0] // cuts
        for i in range(cuts):
            rows = pl.ds(i * size, size)
            at = len(pieces)
            pieces.append((
                pltpu.make_async_copy(src.at[rows], mid.at[rows], sem.at[at]),
                pltpu.make_async_copy(mid.at[rows], dst.at[rows], sem.at[7 + at]),
            ))
    for load, _ in pieces:
        load.start()
    for load, store in pieces:
        load.wait()
        store.start()
    for _, store in pieces:
        store.wait()


def tables(block_rows, block_slots):
    keys = jnp.pad(block_slots * 64 + block_rows, (0, 128), constant_values=-1).reshape(64, 16)
    window = jnp.concatenate([keys[i : i + 60] for i in range(4)] * 2, axis=1)
    return window


def body(tokens, cotangent, weight_blocks, block_rows, block_slots):
    window = tables(block_rows, block_slots)
    vm = pl.BlockSpec(memory_space=pltpu.VMEM)
    sm = pl.BlockSpec(memory_space=pltpu.SMEM)
    hb = pl.BlockSpec(memory_space=pl.ANY)
    sem = pltpu.SemaphoreType.DMA
    call = pl.pallas_call(
        kernel,
        out_shape=(
            jax.ShapeDtypeStruct((T, COLS), BF),
            jax.ShapeDtypeStruct((T, F), BF),
            jax.ShapeDtypeStruct((KEPT, 128), F32),
        ),
        in_specs=[vm, hb, hb, vm, sm],
        out_specs=(hb, hb, vm),
        scratch_shapes=[
            pltpu.VMEM((T, COLS), BF),
            pltpu.VMEM((T, F), BF),
            pltpu.SMEM((SLOTS,), jnp.int32),
            pltpu.VMEM((KEPT, 256), BF),
            pltpu.VMEM((SLOTS * 64, 256), BF),
            pltpu.VMEM((GROUPS + 4, 16, 512), BF),
            pltpu.VMEM((GROUPS + 4, 16, 512), BF),
            pltpu.VMEM((8, 32, 16, COLS), BF),
            pltpu.VMEM((4, T, COLS), BF),
            pltpu.VMEM((8, 4, T, 128), BF),
            pltpu.VMEM((8, 3, T, 128), BF),
            pltpu.VMEM((NZ, 8, 16, 4 * T), BF),
            pltpu.VMEM((NZ, 128, COLS), F32),
            pltpu.VMEM((2, SLOTS, 64, 256), BF),
            pltpu.VMEM((8, KEPT, 128), BF),
            pltpu.VMEM((4, KEPT, 128), BF),
            pltpu.VMEM((4, KEPT, 128), BF),
            pltpu.VMEM((8, F, T), BF),
            pltpu.VMEM((4, F, T), BF),
            pltpu.VMEM((3, F, T), BF),
            sem((3,)),
            sem((12,)), sem((12,)),
            sem((3,)), sem((3,)),
            sem((3,)), sem((3,)),
            sem((4,)), sem((4,)),
            sem((3,)), sem((3,)),
            sem((4,)), sem((4,)),
            sem((1,)), sem((1,)),
            sem((3,)), sem((3,)),
            sem((16,)), sem((16,)),
            sem((16,)), sem((16,)),
        ],
        compiler_params=pltpu.CompilerParams(
            collective_id=0, has_side_effects=True, vmem_limit_bytes=62 * 2**20
        ),
        cost_estimate=pl.CostEstimate(flops=14_000_000_000, bytes_accessed=12_000_000, transcendentals=0),
    )
    outs = call(tokens, cotangent, weight_blocks.reshape(GROUPS, 16, 4096), window, block_slots)
    place = pl.pallas_call(
        place_kernel,
        out_shape=[jax.ShapeDtypeStruct(o.shape, o.dtype) for o in outs],
        in_specs=[hb] * 3,
        out_specs=[hb] * 3,
        scratch_shapes=[pltpu.VMEM(o.shape, o.dtype) for o in outs] + [sem((14,))],
    )
    return tuple(place(*outs))


def solution(mesh):
    placed = (P("dp", "tensor"), P("dp", "tensor"), P("tensor", None), P("tensor"), P("tensor"))
    return jax.shard_map(
        body,
        mesh=mesh,
        in_specs=placed,
        out_specs=(P("dp", "tensor"), P("dp", "tensor"), P("tensor", "dp")),
        check_vma=False,
    )
```

```python
import functools

import jax
import jax.numpy as jnp
from jax import lax
from jax.experimental import pallas as pl
from jax.experimental.pallas import tpu as pltpu
from jax.sharding import PartitionSpec as P

MESH = pl.DeviceIdType.MESH
BF = jnp.bfloat16
F32 = jnp.float32

NX, NZ, NY = 4, 8, 4
T = 256
F = 512
SLOTS = 34
PAIRS = 17
COLS = 2176
KEPT = 896
GROUPS = 56
QUARTER = KEPT // 4
EARLY = 1664
REL_ORDER = (0, 1, 3, 2)


def dot(a, b):
    return jnp.dot(a, b, preferred_element_type=F32)


def dot_nt(a, b):
    return lax.dot_general(a, b, (((1,), (1,)), ((), ())), preferred_element_type=F32)


def square(v):
    w = v.astype(F32)
    return (w * w).astype(BF)


def kernel(
    tok, cot_hbm, wb_hbm, windows, slots,
    hid_out, grads_out, curv,
    hid, grads, slot_first, pick, onehot, wb0, wb1, w, cotv, xf, xq, x2t, acc, gbuf, y, rp, rm, bp, bcore, by,
    loc_sem, xs, xr, a_s, ar, ts, tr, tcs, tcr, qs, qr, qcs, qcr, bcs, bcr, bys, byr, zps, zpr, zms, zmr,
):
    dp = lax.axis_index("dp")
    te = lax.axis_index("tensor")
    px = dp // NZ
    pz = lax.rem(dp, NZ)
    py = te // 2
    pc = lax.rem(te, 2)

    def at_x(d):
        return (lax.rem(px + d, NX) * NZ + pz, te)

    def at_z(d):
        return (px * NZ + lax.rem(pz + d, NZ), te)

    def at_y(d):
        return (dp, lax.rem(py + d, NY) * 2 + pc)

    other = (dp, py * 2 + (1 - pc))

    def send(src, dst, ssem, rsem, where):
        return pltpu.make_async_remote_copy(
            src_ref=src, dst_ref=dst, send_sem=ssem, recv_sem=rsem,
            device_id=where, device_id_type=MESH,
        )

    load_cot = pltpu.make_async_copy(cot_hbm, cotv.at[0], loc_sem.at[0])
    load_cot.start()

    def load_wb(kk, slot):
        return pltpu.make_async_copy(
            wb_hbm.at[:, :, pl.ds(pl.multiple_of(kk * 512, 512), 512)],
            (wb0, wb1)[slot].at[pl.ds(0, GROUPS)],
            loc_sem.at[1 + slot],
        )

    load_wb(0, 0).start()
    load_wb(1, 1).start()

    barrier = pltpu.get_barrier_semaphore()
    peers = [at_x(1), at_x(2), at_x(3), at_y(1), at_y(2), at_y(3), other, at_z(1), at_z(7)]
    for who in peers:
        pl.semaphore_signal(barrier, inc=1, device_id=who, device_id_type=MESH)

    fi = lax.broadcasted_iota(jnp.int32, (F, F), 0)
    ci = lax.broadcasted_iota(jnp.int32, (F, F), 1)
    perm = ((fi // 64 == ci % 8) & (fi % 64 == ci // 8)).astype(F32).astype(BF)
    xp = dot(tok[...], perm).astype(BF)
    for q in range(4):
        xf[te, q] = xp[:, q * 128 : (q + 1) * 128]
    wb0[GROUPS:, :, :] = jnp.zeros((4, 16, 512), BF)
    wb1[GROUPS:, :, :] = jnp.zeros((4, 16, 512), BF)

    pl.semaphore_wait(barrier, len(peers))

    a2a = []
    for d in (1, 2, 3):
        a2a.append(send(xf.at[te, lax.rem(px + d, NX)], xq.at[te, 3 - d], a_s.at[3 - d], ar.at[3 - d], at_x(d)))
    for c in a2a:
        c.start()
    tok_y = [send(xf.at[te], xf.at[te], ts.at[d - 1], tr.at[d - 1], at_y(d)) for d in (1, 2, 3)]
    for c in tok_y:
        c.start()
    tok_core = [send(xf.at[te], xf.at[te], tcs.at[0], tcr.at[0], other)]
    tok_core[0].start()

    load_cot.wait()
    parts = [pl.ds(i * 64, 64) for i in range(4)]
    cx = []

    def send_part(i):
        at = len(cx)
        cx.append(send(cotv.at[0, parts[i]], cotv.at[3, parts[i]], xs.at[at], xr.at[at], at_x(1)))
        cx[-1].start()
        at += 1
        cx.append(send(cotv.at[0, parts[3 - i]], cotv.at[1, parts[3 - i]], xs.at[at], xr.at[at], at_x(3)))
        cx[-1].start()

    send_part(0)
    send_part(1)

    lane = lax.broadcasted_iota(jnp.int32, (1, 128), 1)

    def slot_step(s, at):
        slot_first[s] = at
        here = slots[jnp.minimum(at, GROUPS - 1) * 16]
        there = slots[jnp.minimum(at + 1, GROUPS - 1) * 16]
        one = (at < GROUPS) & (here == s)
        three = (at + 1 < GROUPS) & (there == s)
        return at + jnp.where(one, jnp.where(three, 3, 1), 0)

    lax.fori_loop(0, SLOTS, slot_step, jnp.int32(0))

    def pick_step(v, carry):
        k = jnp.where(lane < 64, windows[pl.ds(v * 8, 1), :], windows[pl.ds(v * 8 + 4, 1), :])
        wanted = lax.rem(lane, 64) // 16 * 64 + lax.rem(k, 64)
        e = (lax.broadcasted_iota(jnp.int32, (256, 128), 0) == wanted).astype(F32)
        pick[pl.ds(pl.multiple_of(v * 128, 128), 128), :] = e.T.astype(BF)
        return carry

    def place_rows(q, ns):
        parts = []
        for i in range(0, ns, 2):
            s = q * 4 + i
            k0 = windows[pl.ds(slot_first[s], 1), :] - s * 64
            k1 = windows[pl.ds(slot_first[s + 1], 1), :] - (s * 64 + 64)
            k = jnp.where(lane < 64, k0, k1)
            base = jnp.where(lane < 64, i * 64, i * 64 + 64)
            parts.append(jnp.where((k >= 0) & (k < 64), k + base, -1))
        wanted = jnp.concatenate(parts, axis=1) if len(parts) > 1 else parts[0]
        n = ns * 64
        e = (lax.broadcasted_iota(jnp.int32, (n, n), 0) == wanted).astype(F32).astype(BF)
        onehot[pl.ds(pl.multiple_of(q * 256, 256), n), pl.ds(0, n)] = e

    def place_step(q, carry):
        place_rows(q, 4)
        return carry

    lax.fori_loop(0, 8, place_step, 0)
    place_rows(8, 2)

    low = lax.broadcasted_iota(jnp.int32, (64, 128), 1) < 64

    def expand_group(q, ns, kk, slot):
        lhs = onehot[pl.ds(pl.multiple_of(q * 256, 256), ns * 64), pl.ds(0, ns * 64)]
        buf = (wb0, wb1)[slot]
        firsts = [slot_first[q * 4 + i] for i in range(ns)]
        for side in range(2):
            rhs = jnp.concatenate(
                [buf[pl.ds(first, 4), :, pl.ds(side * 256, 256)].reshape(64, 256) for first in firsts], axis=0
            )
            out = dot(lhs, rhs)
            for pair in range(ns // 2):
                for k2 in range(2):
                    a = out[pair * 128 : pair * 128 + 64, k2 * 128 : k2 * 128 + 128]
                    b = out[pair * 128 + 64 : pair * 128 + 128, k2 * 128 : k2 * 128 + 128]
                    p0 = jnp.where(low, a, pltpu.roll(b, 64, 1)).reshape(8, 1, 8, 128)
                    p1 = jnp.where(low, pltpu.roll(a, 64, 1), b).reshape(8, 1, 8, 128)
                    tile = jnp.concatenate([p0, p1], axis=1).reshape(8, 16, 128).astype(BF)
                    w[:, kk * 4 + side * 2 + k2, :, pl.ds(pl.multiple_of(q * 256 + pair * 128, 128), 128)] = tile

    def expand_step(kk, slot):
        load_wb(kk, slot).wait()

        def group(q, carry):
            expand_group(q, 4, kk, slot)
            return carry

        lax.fori_loop(0, 8, group, 0, unroll=2)
        expand_group(8, 2, kk, slot)

    def expand_two(i, carry):
        for slot in range(2):
            expand_step(i * 2 + slot, slot)
            load_wb(i * 2 + 2 + slot, slot).start()
        return carry

    lax.fori_loop(0, 2, expand_two, 0)

    cx[0].wait_send()
    cx[1].wait_send()
    send_part(2)

    for c in a2a:
        c.wait_recv()
    xq_y = [send(xq.at[te], xq.at[te], qs.at[d - 1], qr.at[d - 1], at_y(d)) for d in (1, 2, 3)]
    for c in xq_y:
        c.start()
    xq_core = [send(xq.at[te], xq.at[te], qcs.at[0], qcr.at[0], other)]
    xq_core[0].start()

    lax.fori_loop(2, 3, expand_two, 0)
    for slot in range(2):
        expand_step(6 + slot, slot)

    def relay(buf, copies, core, ssem, rsem):
        for d in (1, 2, 3):
            copies[d - 1].wait_recv()
            src = lax.rem(py + NY - d, NY) * 2 + pc
            c = send(buf.at[src], buf.at[src], ssem.at[d], rsem.at[d], other)
            c.start()
            core.append(c)

    cx[2].wait_send()
    cx[3].wait_send()
    send_part(3)

    relay(xf, tok_y, tok_core, tcs, tcr)

    def back(j, carry):
        part = dot_nt(w[pl.ds(j * 2, 2)].reshape(2 * F, COLS), cotv[0]).astype(BF)
        bp[j] = part[:F]
        bp[4 + j] = part[F:]
        return carry

    lax.fori_loop(0, 4, back, 0)
    b_core = send(bp.at[pl.ds((1 - pc) * 4, 4)], bcore, bcs.at[0], bcr.at[0], other)
    b_core.start()

    for c in cx[:4]:
        c.wait_recv()
    fwd = []

    def forward(columns):
        for up in (True, False):
            rel, rows, to = (3, pl.ds(0, 128), at_x(1)) if up else (1, pl.ds(128, 128), at_x(3))
            at = 8 + len(fwd)
            fwd.append(send(cotv.at[rel, rows, columns], cotv.at[2, rows, columns], xs.at[at], xr.at[at], to))
            fwd[-1].start()

    forward(pl.ds(0, EARLY))

    relay(xq, xq_y, xq_core, qcs, qcr)

    for c in tok_core:
        c.wait_recv()

    def hidden_tile(start, width):
        lhs = jnp.concatenate([xf[j, q] for j in range(8) for q in range(4)], axis=1)
        rhs = w[:, :, :, pl.ds(start, width)].reshape(4096, width)
        hid[:, pl.ds(start, width)] = dot(lhs, rhs).astype(BF)

    def hidden_step(n, carry):
        hidden_tile(pl.multiple_of(n * 256, 256), 256)
        return carry

    lax.fori_loop(0, 2, hidden_step, 0)
    lax.fori_loop(0, 7, pick_step, 0)

    b_core.wait_recv()
    b_y = []
    for d in (1, 2, 3):
        to = lax.rem(py + d, NY)
        total = bp[pc * 4 + to].astype(F32) + bcore[to].astype(F32)
        bp[pc * 4 + to] = total.astype(BF)
        c = send(bp.at[pc * 4 + to], by.at[d - 1], bys.at[d - 1], byr.at[d - 1], at_y(d))
        c.start()
        b_y.append(c)

    for c in xq_core:
        c.wait_recv()

    def put_square(j, rel, slab):
        at = REL_ORDER.index(rel)
        v = slab.astype(F32)
        v = (v * v).T.astype(BF)
        x2t[:, j, :, pl.ds(at * T, T)] = v.reshape(NZ, 16, T)

    def squares(j, carry):
        put_square(j, 0, xf[j, px])
        for d in (1, 2, 3):
            put_square(j, d, xq[j, d - 1])
        return carry

    lax.fori_loop(0, 8, squares, 0)

    for c in cx[4:]:
        c.wait_recv()

    def outer_tile(start, width):
        lhs = x2t[:, :, :, pl.ds(0, 3 * T)].reshape(1024, 3 * T)
        rhs = jnp.concatenate([square(cotv[r, :, pl.ds(start, width)]) for r in REL_ORDER[:3]], axis=0)
        acc[:, :, pl.ds(start, width)] = dot(lhs, rhs).reshape(NZ, 128, width)

    def outer_step(n, carry):
        outer_tile(pl.multiple_of(n * 256, 256), 256)
        return carry

    lax.fori_loop(0, 8, outer_step, 0)
    outer_tile(2048, 128)

    for c in fwd[:2]:
        c.wait_send()
    forward(pl.ds(EARLY, COLS - EARLY))

    def square_last(start, width):
        def step(i, carry):
            at = (2, pl.ds(pl.multiple_of(i * 64, 64), 64), pl.ds(start, width))
            cotv[at] = square(cotv[at])
            return carry

        lax.fori_loop(0, 4, step, 0)

    def rearrange(g, da, db, start, width):
        at = [lax.rem(pz + d, NZ) for d in (da, db)]
        lhs = jnp.concatenate([x2t[z, :, :, pl.ds(3 * T, T)].reshape(128, T) for z in at], axis=0)
        last = dot(lhs, cotv[2, :, pl.ds(start, width)])
        for side in range(2):
            whole = acc[at[side], :, pl.ds(start, width)] + last[side * 128 : side * 128 + 128]
            for pair in range(width // 128):
                o = whole[:, pair * 128 : pair * 128 + 128].reshape(8, 2, 8, 128)
                p0 = o[:, 0].reshape(64, 128)
                p1 = o[:, 1].reshape(64, 128)
                a = jnp.where(low, p0, pltpu.roll(p1, 64, 1))
                b = jnp.where(low, pltpu.roll(p0, 64, 1), p1)
                slot = start // 64 + pair * 2
                gbuf[g, slot, :, side * 128 : side * 128 + 128] = a.astype(BF)
                gbuf[g, slot + 1, :, side * 128 : side * 128 + 128] = b.astype(BF)

    def chunks(g, da, db, columns, windows_of):
        def rearrange_step(n, carry):
            rearrange(g, da, db, pl.multiple_of(n * 256, 256), 256)
            return carry

        first, end = columns
        lax.fori_loop((first + 255) // 256, end // 256, rearrange_step, 0, unroll=2)
        if first % 256:
            rearrange(g, da, db, first, 128)
        if end % 256:
            rearrange(g, da, db, end - 128, 128)

        def window(i, carry):
            rhs = jnp.concatenate([gbuf[g, slots[(i * 4 + k) * 16]] for k in range(4)], axis=0)
            rows = pl.ds(pl.multiple_of(i * 64, 64), 64)
            out = dot(pick[rows, :], rhs).astype(BF)
            y[da, rows, :] = out[:, :128]
            y[db, rows, :] = out[:, 128:]
            return carry

        lax.fori_loop(*windows_of, window, 0, unroll=7)

    rows_of = [pl.ds(i * QUARTER, QUARTER) for i in range(4)]
    sent = {}

    def z_step(up, step, h):
        d = 4 - step if up else 4 + step
        buf, ssem, rsem, to = (rp, zps, zpr, at_z(1)) if up else (rm, zms, zmr, at_z(7))
        rows = rows_of[h]
        if (up, step - 1, h) in sent:
            sent[(up, step - 1, h)].wait_recv()
            y[d, rows, :] = (y[d, rows, :].astype(F32) + buf[step - 1, rows, :].astype(F32)).astype(BF)
        at = step * 4 + h
        c = send(y.at[d, rows], buf.at[step, rows], ssem.at[at], rsem.at[at], to)
        c.start()
        sent[(up, step, h)] = c

    def z_steps(up, step, parts_of):
        for h in parts_of:
            z_step(up, step, h)

    early, late, every = (0, EARLY), (EARLY, COLS), (0, COLS)
    half_a, half_b, both = (0, 7), (7, 14), (0, 14)
    for c in fwd[:2]:
        c.wait_recv()
    square_last(0, EARLY)
    chunks(0, 4, 3, early, half_a)
    z_step(True, 0, 0)
    z_step(False, 0, 1)
    z_step(True, 1, 1)
    chunks(1, 5, 2, early, half_a)
    z_step(False, 1, 0)
    for c in fwd[2:]:
        c.wait_recv()
    square_last(EARLY, COLS - EARLY)
    chunks(0, 4, 3, late, half_b)
    z_step(True, 0, 2)
    z_step(False, 0, 3)
    z_step(True, 1, 3)
    chunks(1, 5, 2, late, half_b)
    z_step(False, 1, 2)
    z_step(True, 1, 0)
    z_step(False, 1, 1)
    z_step(True, 1, 2)
    z_step(False, 1, 3)
    chunks(0, 6, 1, every, both)
    for h in (1, 0, 3, 2):
        z_step(True, 2, h)
        z_step(False, 2, h ^ 1)
    chunks(1, 7, 0, every, both)
    lax.fori_loop(2, 5, hidden_step, 0)
    for h in (1, 0, 3, 2):
        z_step(True, 3, h)
        z_step(False, 3, h ^ 1)
    lax.fori_loop(5, 8, hidden_step, 0)
    hidden_tile(2048, 128)
    store_hid = pltpu.make_async_copy(hid, hid_out, loc_sem.at[0])
    store_hid.start()

    total = bp[pc * 4 + py].astype(F32) + bcore[py].astype(F32)
    for d in (1, 2, 3):
        b_y[d - 1].wait_recv()
        total = total + by[d - 1].astype(F32)
    grads[...] = dot(perm, total.astype(BF)).T.astype(BF)
    store_grads = pltpu.make_async_copy(grads, grads_out, loc_sem.at[1])
    store_grads.start()

    for h in (1, 0, 3, 2):
        sent[(True, 3, h)].wait_recv()
        sent[(False, 3, h)].wait_recv()
        value = (
            y[0, rows_of[h], :].astype(F32)
            + rp[3, rows_of[h], :].astype(F32)
            + rm[3, rows_of[h], :].astype(F32)
        )
        curv[rows_of[h], :] = value * (1.0 / 8192.0)

    store_hid.wait()
    store_grads.wait()
    for c in a2a + tok_y + tok_core + cx[4:] + xq_y + xq_core + fwd[2:] + [b_core] + b_y + list(sent.values()):
        c.wait_send()


def place_kernel(a, b, c, oa, ob, oc, va, vb, vc, sem):
    pieces = []
    for src, mid, dst, cuts in ((a, va, oa, 4), (c, vc, oc, 2), (b, vb, ob, 1)):
        size = src.shape[0] // cuts
        for i in range(cuts):
            rows = pl.ds(i * size, size)
            at = len(pieces)
            pieces.append((
                pltpu.make_async_copy(src.at[rows], mid.at[rows], sem.at[at]),
                pltpu.make_async_copy(mid.at[rows], dst.at[rows], sem.at[7 + at]),
            ))
    for load, _ in pieces:
        load.start()
    for load, store in pieces:
        load.wait()
        store.start()
    for _, store in pieces:
        store.wait()


def tables(block_rows, block_slots):
    keys = jnp.pad(block_slots * 64 + block_rows, (0, 128), constant_values=-1).reshape(64, 16)
    window = jnp.concatenate([keys[i : i + 60] for i in range(4)] * 2, axis=1)
    return window


def body(tokens, cotangent, weight_blocks, block_rows, block_slots):
    window = tables(block_rows, block_slots)
    vm = pl.BlockSpec(memory_space=pltpu.VMEM)
    sm = pl.BlockSpec(memory_space=pltpu.SMEM)
    hb = pl.BlockSpec(memory_space=pl.ANY)
    sem = pltpu.SemaphoreType.DMA
    call = pl.pallas_call(
        kernel,
        out_shape=(
            jax.ShapeDtypeStruct((T, COLS), BF),
            jax.ShapeDtypeStruct((T, F), BF),
            jax.ShapeDtypeStruct((KEPT, 128), F32),
        ),
        in_specs=[vm, hb, hb, vm, sm],
        out_specs=(hb, hb, vm),
        scratch_shapes=[
            pltpu.VMEM((T, COLS), BF),
            pltpu.VMEM((T, F), BF),
            pltpu.SMEM((SLOTS,), jnp.int32),
            pltpu.VMEM((KEPT, 256), BF),
            pltpu.VMEM((SLOTS * 64, 256), BF),
            pltpu.VMEM((GROUPS + 4, 16, 512), BF),
            pltpu.VMEM((GROUPS + 4, 16, 512), BF),
            pltpu.VMEM((8, 32, 16, COLS), BF),
            pltpu.VMEM((4, T, COLS), BF),
            pltpu.VMEM((8, 4, T, 128), BF),
            pltpu.VMEM((8, 3, T, 128), BF),
            pltpu.VMEM((NZ, 8, 16, 4 * T), BF),
            pltpu.VMEM((NZ, 128, COLS), F32),
            pltpu.VMEM((2, SLOTS, 64, 256), BF),
            pltpu.VMEM((8, KEPT, 128), BF),
            pltpu.VMEM((4, KEPT, 128), BF),
            pltpu.VMEM((4, KEPT, 128), BF),
            pltpu.VMEM((8, F, T), BF),
            pltpu.VMEM((4, F, T), BF),
            pltpu.VMEM((3, F, T), BF),
            sem((3,)),
            sem((12,)), sem((12,)),
            sem((3,)), sem((3,)),
            sem((3,)), sem((3,)),
            sem((4,)), sem((4,)),
            sem((3,)), sem((3,)),
            sem((4,)), sem((4,)),
            sem((1,)), sem((1,)),
            sem((3,)), sem((3,)),
            sem((16,)), sem((16,)),
            sem((16,)), sem((16,)),
        ],
        compiler_params=pltpu.CompilerParams(
            collective_id=0, has_side_effects=True, vmem_limit_bytes=62 * 2**20
        ),
        cost_estimate=pl.CostEstimate(flops=14_000_000_000, bytes_accessed=12_000_000, transcendentals=0),
    )
    outs = call(tokens, cotangent, weight_blocks.reshape(GROUPS, 16, 4096), window, block_slots)
    place = pl.pallas_call(
        place_kernel,
        out_shape=[jax.ShapeDtypeStruct(o.shape, o.dtype) for o in outs],
        in_specs=[hb] * 3,
        out_specs=[hb] * 3,
        scratch_shapes=[pltpu.VMEM(o.shape, o.dtype) for o in outs] + [sem((14,))],
    )
    return tuple(place(*outs))


def solution(mesh):
    placed = (P("dp", "tensor"), P("dp", "tensor"), P("tensor", None), P("tensor"), P("tensor"))
    return jax.shard_map(
        body,
        mesh=mesh,
        in_specs=placed,
        out_specs=(P("dp", "tensor"), P("dp", "tensor"), P("tensor", "dp")),
        check_vma=False,
    )
```
